256 devices in a mesh: row: 16 (over z, core), col: 16 (over y, x).
Axes of the slice: x: 4, y: 4, z: 8, core: 2. Of those that a mesh axis runs over, the one named last changes fastest.
Arguments:
- features: bfloat16 [131072, 256], P(('col', 'row')), may hold values from -0.0625 to 0.0625
- weight: bfloat16 [256, 256], replicated, may hold values from -0.375 to 0.375
- pre_act: bfloat16 [131072, 256], P('row', 'col'), may hold values from -6 to 6
- grad_out: bfloat16 [131072, 256], P('row', 'col'), may hold values from -6 to 6
- tile_ids: int32 [16, 16, 320], P('row', 'col'), may hold values from 0 to 4095, as said below
- tile_count: int32 [16, 16], P('row', 'col'), may hold values from 1 to 320
- tile_values: bfloat16 [16, 16, 320, 128, 128], P('row', 'col'), may hold values from -0.078125 to 0.078125
Outputs:
- grad_in: bfloat16 [131072, 256], P(('col', 'row'))
- grad_weight: float32 [256, 256], P('row', 'col')
The draws below stay inside these ranges and needn't reach their ends.
Inputs may be any that keep to these rules, and one draw needn't show every extreme that they name: `tile_ids`: the entries of one grid cell's list are distinct; slots from tile_count on are not used.
All inputs are finite; a program needn't handle non-finite values.
Results may differ from the reference program's by a relative error of at most 0.005.
Values may be sent and summed in bfloat16 or wider, within the bound.
No kernel may reach another device: no remote copies, remote signals or barrier semaphores. Data moves between devices by JAX's collectives and lax.ppermute only.
A program may use at most 128 MiB of HBM per device.

```python
import jax
import jax.numpy as jnp
from jax import lax

F = 256
BPD = 4
TILES_DEV = 320
ROW_TILES = 64
COL_TILES = 64
NODES = 131072
N_ROW = 16
N_COL = 16


def draw_tile_ids(key, part):
    key = jax.random.fold_in(key, 11)
    total = ROW_TILES * COL_TILES
    cells = N_ROW * N_COL
    cell_keys = jax.random.split(jax.random.fold_in(key, 1), cells)

    def one_perm(cell_key):
        return jax.random.permutation(cell_key, total)[:TILES_DEV]
    perms = jax.vmap(one_perm)(cell_keys).astype(jnp.int32)
    pick_cell = jax.random.randint(jax.random.fold_in(key, 2), (), 0, cells)
    pick_slot = jax.random.randint(jax.random.fold_in(key, 3), (), 0, TILES_DEV)
    shift = (total - 1 - perms[pick_cell, pick_slot]) % total
    offsets = jnp.where(jnp.arange(cells, dtype=jnp.int32) == pick_cell, shift, 0).astype(jnp.int32)
    tile_list = (perms + offsets[:, None]) % total
    return tile_list.reshape(N_ROW, N_COL, TILES_DEV).astype(jnp.int32)


def draw_tile_count(key, part):
    key = jax.random.fold_in(key, 23)
    cells = N_ROW * N_COL
    divisors = jax.random.randint(jax.random.fold_in(key, 1), (cells,), 1, 7)
    counts = jnp.maximum(TILES_DEV // divisors, 1)
    pick_cell = jax.random.randint(jax.random.fold_in(key, 2), (), 0, cells)
    counts = jnp.where(jnp.arange(cells, dtype=jnp.int32) == pick_cell, TILES_DEV, counts)
    return counts.reshape(N_ROW, N_COL).astype(jnp.int32)


def raised(array, own_key, source, target, shards_of, factor):
    def block_of(position):
        return (jnp.arange(array.shape[position]) // (array.shape[position] // shards_of)).reshape((-1,) + (1,) * (array.ndim - 1 - position))

    near = jax.random.permutation(own_key, shards_of)[block_of(target)]
    other_side = (block_of(target) + shards_of // 2) % shards_of
    return jnp.where((block_of(source) == near) | (block_of(source) == other_side), factor * array, array)


def steps_of(rng, dims, shards, low, high):
    def one(axis_at, parts):
        steps = jax.random.uniform(jax.random.fold_in(jax.random.fold_in(rng, 6), axis_at), (parts,), jnp.float32, low / len(shards), high / len(shards))
        return jnp.repeat(jnp.exp(steps), dims[axis_at] // parts).reshape((-1,) + (1,) * (len(dims) - axis_at - 1))

    gain = one(*shards[0])
    for cut in shards[1:]:
        gain = gain * one(*cut)
    return gain


def centred(own_key, dims, deviation, limit, shards=(), kind=jnp.bfloat16):
    values = deviation * jax.random.normal(own_key, dims, jnp.float32)
    if shards:
        values = values * steps_of(own_key, dims, shards, -0.22, 0.18)
    return jnp.clip(values, -limit, limit).astype(kind)


def heavy_noise(key, shape, deviation, bound, cuts, heavy, held_as=jnp.bfloat16):
    values = deviation * jax.random.normal(key, shape, jnp.float32)
    if cuts:
        values = values * steps_of(key, shape, cuts, -0.22, 0.18)
    return jnp.clip(raised(values, jax.random.fold_in(key, 3), *heavy), -bound, bound).astype(held_as)


def setup_inputs(seed: int = 0) -> dict:
    streams_of = jax.random.split(jax.random.key(seed), 8)
    return {
        "features": heavy_noise(streams_of[0], (NODES, F), NODES ** -0.5, 0.0625, ((0, 256),), (0, 1, 256, 6.0)),
        "weight": centred(streams_of[1], (F, F), F ** -0.5, 0.375),
        "pre_act": centred(streams_of[2], (NODES, F), 1.0, 6.0, ((0, 16), (1, 16))),
        "grad_out": centred(streams_of[3], (NODES, F), 1.0, 6.0, ((0, 16), (1, 16))),
        "tile_ids": draw_tile_ids(jax.random.fold_in(streams_of[7], 71), 0),
        "tile_count": draw_tile_count(jax.random.fold_in(streams_of[7], 71), 0),
        "tile_values": centred(streams_of[6], (N_ROW, N_COL, TILES_DEV, 128, 128), (64 * TILES_DEV // BPD) ** -0.5, 0.078125, ((0, 16), (1, 16))),
    }


def reference(features, weight, pre_act, grad_out, tile_ids, tile_count, tile_values):
    grad_pre = jnp.where(pre_act > 0, grad_out, jnp.zeros_like(grad_out))
    row_nodes = 128 * ROW_TILES
    cells = N_ROW * N_COL

    def one_cell(running, cell_index):
        row_index = cell_index // N_COL
        col_index = cell_index % N_COL
        tile_list = tile_ids[row_index, col_index]
        values = tile_values[row_index, col_index].astype(jnp.float32)
        live_tiles = tile_count[row_index, col_index]
        block = lax.dynamic_slice_in_dim(grad_pre, (row_index * row_nodes).astype(jnp.int32), row_nodes, 0)
        source = block.reshape(ROW_TILES, 128, F).astype(jnp.float32)
        picked = source[tile_list // COL_TILES]
        product = jnp.einsum("tkn,tkf->tnf", values, picked)
        is_live = jnp.arange(TILES_DEV, dtype=jnp.int32) < live_tiles
        product = jnp.where(is_live[:, None, None], product, jnp.zeros_like(product))
        cell_sum = jnp.zeros((COL_TILES, 128, F), jnp.float32).at[tile_list % COL_TILES].add(product)
        running = running.at[col_index].add(cell_sum)
        return running, None

    start_sum = jnp.zeros((N_COL, COL_TILES, 128, F), jnp.float32)
    summed, _ = lax.scan(one_cell, start_sum, jnp.arange(cells, dtype=jnp.int32))
    spread = summed.reshape(NODES, F).astype(jnp.bfloat16)
    grad_in = jnp.dot(spread, weight.T, preferred_element_type=jnp.float32).astype(jnp.bfloat16)
    grad_weight = jnp.dot(features.T, spread, preferred_element_type=jnp.float32)
    return grad_in, grad_weight
```

```python
import functools

import jax
import jax.numpy as jnp
from jax import lax
from jax.experimental import pallas as pl
from jax.experimental.pallas import tpu as pltpu
from jax.sharding import PartitionSpec as P

BF = jnp.bfloat16
F32 = jnp.float32
TILE = 128
NX = 4
NY = 4
NZ = 8
COLS = 64
STAGES = 4
STAGE_COLS = COLS // STAGES
GROUP = 4
VMEM_LIMIT = 24 * 1024 * 1024


def shift_x(array, step):
    pairs = [(i, (i // NX) * NX + (i % NX + step) % NX) for i in range(NX * NY)]
    return lax.ppermute(array, "col", pairs)


def shift_y(array, step):
    pairs = [(i, (i + NX * step) % (NX * NY)) for i in range(NX * NY)]
    return lax.ppermute(array, "col", pairs)


def shift_z(array, step):
    pairs = [(i, (i + 2 * step) % (2 * NZ)) for i in range(2 * NZ)]
    return lax.ppermute(array, "row", pairs)


def swap_core(array):
    return lax.ppermute(array, "row", [(i, i ^ 1) for i in range(2 * NZ)])


def line_by_hops(shift, block):
    ahead, behind = shift(block, -1), shift(block, 1)
    half = block.shape[0] // 2
    return block, ahead, shift(behind[:half], 1), shift(ahead[half:], -1), behind


def line(shift, block):
    return block, shift(block, -1), shift(block, 2), shift(block, 1)


def pair_kernel(ids_ref, count_ref, info_ref, values_hbm, table_ref, values_ref, value_sem):
    copy = pltpu.make_async_copy(values_hbm, values_ref, value_sem)
    copy.start()
    slots = ids_ref.shape[1]
    room = table_ref.shape[1]
    ids = jnp.broadcast_to(ids_ref[...], (8, slots))
    slot = lax.broadcasted_iota(jnp.int32, (8, slots), 1)
    live = slot < count_ref[0, 0]
    j = ids & (COLS - 1)
    i = lax.shift_right_logical(ids, 6) & (COLS - 1)
    ahead = (lax.shift_right_logical(j, 3) - info_ref[0]) & (NZ - 1)
    is_right = (ahead >= 1) & (ahead <= 4)
    stage = jnp.where(is_right, 4 - ahead, 3 - ((NZ - ahead) & (NZ - 1)))
    rank = stage * STAGE_COLS + jnp.where(is_right, 0, 8) + (j & 7)
    rank = jnp.where(live, rank, -1)

    def flag(mask):
        return jnp.where(mask, 1.0, 0.0).astype(BF)

    def dot(left, right):
        return jnp.dot(left, right, preferred_element_type=F32)

    columns = lax.broadcasted_iota(jnp.int32, (COLS, slots), 0)
    member = columns == rank[:1]
    before = flag(
        lax.broadcasted_iota(jnp.int32, (slots, slots), 0)
        < lax.broadcasted_iota(jnp.int32, (slots, slots), 1)
    )
    earlier = dot(flag(member), before)
    size = jnp.sum(member.astype(F32), axis=1, keepdims=True)
    pairs = jnp.floor((size + 1.0) * 0.5)
    lower = flag(
        lax.broadcasted_iota(jnp.int32, (COLS, COLS), 1)
        < lax.broadcasted_iota(jnp.int32, (COLS, COLS), 0)
    )
    start = dot(lower, jnp.broadcast_to(pairs, (COLS, TILE)).astype(BF))
    spot = jnp.sum(
        jnp.where(member, earlier + 2.0 * start[:, :1], 0.0), axis=0, keepdims=True
    )
    spot = jnp.where(live[:1], spot, -1.0)
    spot = jnp.broadcast_to(spot, (TILE, slots)).T[:, :1]
    target = 2 * lax.broadcasted_iota(jnp.int32, (slots, room), 1)
    row = lax.broadcasted_iota(jnp.int32, (8, slots), 0)
    facts = jnp.where(row == 0, slot // 16, 0)
    facts = jnp.where(row == 1, slot % 16, facts)
    facts = jnp.where(row == 2, i, facts)
    facts = jnp.where(row == 3, rank & (STAGE_COLS - 1), facts)
    facts = jnp.where(row == 4, 1, facts).astype(F32).astype(BF)
    first = dot(facts, flag(spot == target.astype(F32)))
    second = dot(facts, flag(spot == (target + 1).astype(F32)))

    def code(found):
        return ((found[0:1] * 16.0 + found[1:2]) * COLS + found[2:3]).astype(jnp.int32)

    table_ref[0:1] = code(first)
    table_ref[1:2] = jnp.where(second[4:5] > 0.5, code(second), -1)
    table_ref[2:3] = first[3:4].astype(jnp.int32)
    table_ref[3:4] = jnp.zeros((1, room), jnp.int32)
    table_ref[3:4, :COLS] = start.T[0:1].astype(jnp.int32)
    total = jnp.sum(pairs, axis=0, keepdims=True).astype(jnp.int32)
    table_ref[3:4, TILE : 2 * TILE] = jnp.broadcast_to(total, (1, TILE))
    copy.wait()


def list_pairs(tile_ids, tile_count, info, values):
    smem = pl.BlockSpec(memory_space=pltpu.SMEM)
    vmem = pl.BlockSpec(memory_space=pltpu.VMEM)
    room = 256
    return pl.pallas_call(
        pair_kernel,
        in_specs=[vmem, smem, smem, pl.BlockSpec(memory_space=pl.ANY)],
        out_specs=[vmem, vmem],
        out_shape=[
            jax.ShapeDtypeStruct((4, room), jnp.int32),
            jax.ShapeDtypeStruct(values.shape, BF),
        ],
        scratch_shapes=[pltpu.SemaphoreType.DMA],
        compiler_params=pltpu.CompilerParams(vmem_limit_bytes=16 * 1024 * 1024),
        cost_estimate=pl.CostEstimate(flops=0, bytes_accessed=14_000_000, transcendentals=0),
    )(
        tile_ids.reshape(1, -1),
        tile_count,
        info,
        pltpu.with_memory_space_constraint(values, pltpu.HBM),
    )


def tile_kernel(stage, table_ref, info_ref, *refs):
    *pieces, values_ref, mine_ref, other_ref, acc_ref = refs
    core = info_ref[1]
    width = acc_ref.shape[1]
    begin = table_ref[3, stage * STAGE_COLS]
    end = table_ref[3, (stage + 1) * STAGE_COLS if stage < STAGES - 1 else TILE]

    def clear(j, carry):
        acc_ref[j] = jnp.zeros(acc_ref.shape[1:], F32)
        return carry

    lax.fori_loop(0, STAGE_COLS, clear, 0)

    def gathered(code):
        lanes = pl.ds(pl.multiple_of((code & (COLS - 1)) * TILE, TILE), TILE)
        return jnp.concatenate([piece[:, lanes] for piece in pieces], axis=0)

    def group(g, carry):
        for u in range(GROUP):
            pair = begin + g * GROUP + u
            one, two = table_ref[0, pair], table_ref[1, pair]
            both = two >= 0
            two = jnp.maximum(two, 0)
            left_two = jnp.where(both, gathered(two), jnp.zeros((width, TILE), BF))
            left = jnp.concatenate([gathered(one), left_two], axis=1)
            right = jnp.concatenate(
                [
                    values_ref[lax.shift_right_logical(one, 6)],
                    values_ref[lax.shift_right_logical(two, 6)],
                ],
                axis=0,
            )
            dest = jnp.where(pair < end, table_ref[2, pair], STAGE_COLS)
            acc_ref[dest] += jnp.dot(left, right, preferred_element_type=F32)
        return carry

    lax.fori_loop(0, (end - begin + GROUP - 1) // GROUP, group, 0)

    for side in range(2):
        for q in range(4):
            lanes = slice(q * TILE, (q + 1) * TILE)
            mine_ref[side, :, lanes] = acc_ref[side * 8 + core * 4 + q].astype(BF)
            other_ref[side, :, lanes] = acc_ref[side * 8 + (1 - core) * 4 + q].astype(BF)


def tile_products(stage, table, info, pieces, values):
    width = sum(piece.shape[0] for piece in pieces)
    smem = pl.BlockSpec(memory_space=pltpu.SMEM)
    vmem = pl.BlockSpec(memory_space=pltpu.VMEM)
    return pl.pallas_call(
        functools.partial(tile_kernel, stage),
        in_specs=[smem] * 2 + [vmem] * (len(pieces) + 1),
        out_specs=[vmem] * 2,
        scratch_shapes=[pltpu.VMEM((STAGE_COLS + 1, width, TILE), F32)],
        out_shape=[jax.ShapeDtypeStruct((2, width, 512), BF)] * 2,
        compiler_params=pltpu.CompilerParams(vmem_limit_bytes=VMEM_LIMIT),
        cost_estimate=pl.CostEstimate(flops=0, bytes_accessed=1_000_000, transcendentals=0),
    )(table, info, *pieces, values)


def add_bf(*terms):
    return sum(term.astype(F32) for term in terms).astype(BF)


def final_kernel(
    right_ref, left_ref, mine_ref, other_ref, order_ref, weight_ref, feat_ref, grad_ref, term_ref
):
    held = right_ref[...].astype(F32) + left_ref[...].astype(F32)
    held = held + mine_ref[1].astype(F32) + other_ref[1].astype(F32)
    spread = lax.dot_general(
        order_ref[...], held.astype(BF), (((1,), (0,)), ((), ())), preferred_element_type=F32
    ).astype(BF)
    grad_ref[...] = lax.dot_general(
        spread, weight_ref[...], (((0,), (1,)), ((), ())), preferred_element_type=F32
    ).astype(BF)
    term = lax.dot_general(
        feat_ref[...], spread, (((0,), (1,)), ((), ())), preferred_element_type=F32
    )
    rows = lax.broadcasted_iota(jnp.int32, (8, TILE), 0)
    spans = lax.broadcasted_iota(jnp.int32, (8, TILE), 1) // 16
    for half in range(2):
        part = term[:, half * TILE : (half + 1) * TILE].reshape(32, 8, TILE)
        moved = jnp.zeros_like(part)
        for step in range(8):
            turned = part
            if step:
                turned = pltpu.roll(pltpu.roll(part, 8 - step, 1), 16 * step, 2)
            keep = ((spans - rows) & 7) == step
            moved = jnp.where(keep[None], turned, moved)
        for r in range(16):
            for upper in range(2):
                term_ref[
                    r * 16 + half * 8 : r * 16 + half * 8 + 8, upper * TILE : (upper + 1) * TILE
                ] = moved[2 * r + upper]


def finish(right, left, mine, other, order, weight, features):
    return pl.pallas_call(
        final_kernel,
        out_shape=[
            jax.ShapeDtypeStruct(features.shape, BF),
            jax.ShapeDtypeStruct((256, 256), F32),
        ],
        compiler_params=pltpu.CompilerParams(vmem_limit_bytes=16 * 1024 * 1024),
    )(right, left, mine, other, order, weight, features)


def per_device(features, weight, pre_act, grad_out, tile_ids, tile_count, tile_values):
    row = lax.axis_index("row")
    col = lax.axis_index("col")
    x, y = col % NX, col // NX
    z, core = row // 2, row % 2

    pre, grad = pre_act.T, grad_out.T
    masked = jnp.where(pre > 0, grad, jnp.zeros_like(grad))
    half = masked.shape[0] // 2
    along_x = jnp.concatenate(line(shift_x, masked[:half]), axis=0)
    along_y = jnp.concatenate(line(shift_y, masked[half:]), axis=0)

    place = jnp.arange(256, dtype=jnp.int32)
    second = place // 128
    outer, inner = place // 32 % 4, place // 8 % 4
    dy = jnp.where(second == 0, outer, inner)
    dx = jnp.where(second == 0, inner, outer)
    feature = ((y + dy) % NY * NX + (x + dx) % NX) * 16 + second * 8 + place % 8
    order = (place[:, None] == feature[None, :]).astype(BF)

    info = jnp.stack([z, core]).astype(jnp.int32)
    tile_ids, along_x, along_y = lax.optimization_barrier((tile_ids, along_x, along_y))
    table, values = list_pairs(tile_ids, tile_count, info, tile_values[0, 0])
    pieces = line_by_hops(shift_y, along_x) + line_by_hops(shift_x, along_y)

    right, left = [], []
    for stage in range(STAGES):
        mine, other = tile_products(stage, table, info, pieces, values)
        other = swap_core(other)
        right = [shift_z(add_bf(*right, mine[0], other[0]), 1)]
        if stage < STAGES - 1:
            left = [shift_z(add_bf(*left, mine[1], other[1]), -1)]

    grad_in, term = finish(right[0], left[0], mine, other, order, weight, features)
    parts = lax.all_to_all(term, ("row", "col"), 0, 0, tiled=True)
    grad_weight = jnp.sum(parts, axis=0).reshape(16, 16)
    return grad_in, grad_weight


def solution(mesh):
    return jax.shard_map(
        per_device,
        mesh=mesh,
        in_specs=(
            P(("col", "row"), None),
            P(),
            P("row", "col"),
            P("row", "col"),
            P("row", "col", None),
            P("row", "col"),
            P("row", "col", None, None, None),
        ),
        out_specs=(P(("col", "row"), None), P("row", "col")),
        check_vma=False,
    )
```

```python
import functools

import jax
import jax.numpy as jnp
from jax import lax
from jax.experimental import pallas as pl
from jax.experimental.pallas import tpu as pltpu
from jax.sharding import PartitionSpec as P

BF = jnp.bfloat16
F32 = jnp.float32
TILE = 128
NX = 4
NY = 4
NZ = 8
COLS = 64
STAGES = 4
STAGE_COLS = COLS // STAGES
GROUP = 4
VMEM_LIMIT = 20 * 1024 * 1024


def shift_x(array, step):
    pairs = [(i, (i // NX) * NX + (i % NX + step) % NX) for i in range(NX * NY)]
    return lax.ppermute(array, "col", pairs)


def shift_y(array, step):
    pairs = [(i, (i + NX * step) % (NX * NY)) for i in range(NX * NY)]
    return lax.ppermute(array, "col", pairs)


def shift_z(array, step):
    pairs = [(i, (i + 2 * step) % (2 * NZ)) for i in range(2 * NZ)]
    return lax.ppermute(array, "row", pairs)


def swap_core(array):
    return lax.ppermute(array, "row", [(i, i ^ 1) for i in range(2 * NZ)])


def line_by_hops(shift, block):
    ahead, behind = shift(block, -1), shift(block, 1)
    half = block.shape[0] // 2
    return block, ahead, shift(behind[:half], 1), shift(ahead[half:], -1), behind


def line(shift, block):
    return block, shift(block, -1), shift(block, 2), shift(block, 1)


def pair_kernel(ids_ref, count_ref, values_hbm, table_ref, order_ref, values_ref, value_sem):
    copy = pltpu.make_async_copy(values_hbm, values_ref, value_sem)
    copy.start()
    slots = ids_ref.shape[1]
    room = table_ref.shape[1]
    ids = jnp.broadcast_to(ids_ref[...], (8, slots))
    slot = lax.broadcasted_iota(jnp.int32, (8, slots), 1)
    live = slot < count_ref[0, 0]
    j = ids & (COLS - 1)
    i = lax.shift_right_logical(ids, 6) & (COLS - 1)
    ahead = (lax.shift_right_logical(j, 3) - lax.axis_index("row") // 2) & (NZ - 1)
    is_right = (ahead >= 1) & (ahead <= 4)
    stage = jnp.where(is_right, 4 - ahead, 3 - ((NZ - ahead) & (NZ - 1)))
    rank = stage * STAGE_COLS + jnp.where(is_right, 0, 8) + (j & 7)
    rank = jnp.where(live, rank, -1)

    def flag(mask):
        return jnp.where(mask, 1.0, 0.0).astype(BF)

    def dot(left, right):
        return jnp.dot(left, right, preferred_element_type=F32)

    columns = lax.broadcasted_iota(jnp.int32, (COLS, slots), 0)
    member = columns == rank[:1]
    before = flag(
        lax.broadcasted_iota(jnp.int32, (slots, slots), 0)
        < lax.broadcasted_iota(jnp.int32, (slots, slots), 1)
    )
    earlier = dot(flag(member), before)
    size = jnp.sum(member.astype(F32), axis=1, keepdims=True)
    pairs = jnp.floor((size + 1.0) * 0.5)
    lower = flag(
        lax.broadcasted_iota(jnp.int32, (COLS, COLS), 1)
        < lax.broadcasted_iota(jnp.int32, (COLS, COLS), 0)
    )
    start = dot(lower, jnp.broadcast_to(pairs, (COLS, TILE)).astype(BF))
    spot = jnp.sum(
        jnp.where(member, earlier + 2.0 * start[:, :1], 0.0), axis=0, keepdims=True
    )
    spot = jnp.where(live[:1], spot, -1.0)
    spot = jnp.broadcast_to(spot, (TILE, slots)).T[:, :1]
    target = 2 * lax.broadcasted_iota(jnp.int32, (slots, room), 1)
    row = lax.broadcasted_iota(jnp.int32, (8, slots), 0)
    facts = jnp.where(row == 0, slot // 16, 0)
    facts = jnp.where(row == 1, slot % 16, facts)
    facts = jnp.where(row == 2, i, facts)
    facts = jnp.where(row == 3, rank & (STAGE_COLS - 1), facts)
    facts = jnp.where(row == 4, 1, facts).astype(F32).astype(BF)
    first = dot(facts, flag(spot == target.astype(F32)))
    second = dot(facts, flag(spot == (target + 1).astype(F32)))

    def code(found):
        return ((found[0:1] * 16.0 + found[1:2]) * COLS + found[2:3]).astype(jnp.int32)

    table_ref[0:1] = code(first)
    table_ref[1:2] = jnp.where(second[4:5] > 0.5, code(second), -1)
    table_ref[2:3] = first[3:4].astype(jnp.int32)
    table_ref[3:4] = jnp.zeros((1, room), jnp.int32)
    table_ref[3:4, :COLS] = start.T[0:1].astype(jnp.int32)
    total = jnp.sum(pairs, axis=0, keepdims=True).astype(jnp.int32)
    table_ref[3:4, TILE : 2 * TILE] = jnp.broadcast_to(total, (1, TILE))

    col = lax.axis_index("col")
    place = lax.broadcasted_iota(jnp.int32, order_ref.shape, 1)
    second = lax.shift_right_logical(place, 7)
    outer, inner = lax.shift_right_logical(place, 5) & 3, lax.shift_right_logical(place, 3) & 3
    dy = jnp.where(second == 0, outer, inner)
    dx = jnp.where(second == 0, inner, outer)
    device = ((col // NX + dy) & (NY - 1)) * NX + ((col % NX + dx) & (NX - 1))
    feature = device * 16 + second * 8 + (place & 7)
    order_ref[...] = flag(lax.broadcasted_iota(jnp.int32, order_ref.shape, 0) == feature)
    copy.wait()


def list_pairs(tile_ids, tile_count, values):
    smem = pl.BlockSpec(memory_space=pltpu.SMEM)
    vmem = pl.BlockSpec(memory_space=pltpu.VMEM)
    room = 256
    return pl.pallas_call(
        pair_kernel,
        in_specs=[vmem, smem, pl.BlockSpec(memory_space=pl.ANY)],
        out_specs=[vmem] * 3,
        out_shape=[
            jax.ShapeDtypeStruct((4, room), jnp.int32),
            jax.ShapeDtypeStruct((256, 256), BF),
            jax.ShapeDtypeStruct(values.shape, BF),
        ],
        scratch_shapes=[pltpu.SemaphoreType.DMA],
        compiler_params=pltpu.CompilerParams(vmem_limit_bytes=16 * 1024 * 1024),
        cost_estimate=pl.CostEstimate(flops=0, bytes_accessed=14_000_000, transcendentals=0),
    )(
        tile_ids.reshape(1, -1),
        tile_count,
        pltpu.with_memory_space_constraint(values, pltpu.HBM),
    )


def tile_kernel(stage, table_ref, *refs):
    *pieces, values_ref, mine_ref, other_ref, acc_ref = refs
    core = lax.axis_index("row") % 2
    width = acc_ref.shape[1]
    begin = table_ref[3, stage * STAGE_COLS]
    end = table_ref[3, (stage + 1) * STAGE_COLS if stage < STAGES - 1 else TILE]

    def clear(j, carry):
        acc_ref[j] = jnp.zeros(acc_ref.shape[1:], F32)
        return carry

    lax.fori_loop(0, STAGE_COLS, clear, 0)

    def gathered(code):
        lanes = pl.ds(pl.multiple_of((code & (COLS - 1)) * TILE, TILE), TILE)
        return jnp.concatenate([piece[:, lanes] for piece in pieces], axis=0)

    def group(g, carry):
        for u in range(GROUP):
            pair = begin + g * GROUP + u
            one, two = table_ref[0, pair], table_ref[1, pair]
            both = two >= 0
            two = jnp.maximum(two, 0)
            left_two = jnp.where(both, gathered(two), jnp.zeros((width, TILE), BF))
            left = jnp.concatenate([gathered(one), left_two], axis=1)
            right = jnp.concatenate(
                [
                    values_ref[lax.shift_right_logical(one, 6)],
                    values_ref[lax.shift_right_logical(two, 6)],
                ],
                axis=0,
            )
            dest = jnp.where(pair < end, table_ref[2, pair], STAGE_COLS)
            acc_ref[dest] += jnp.dot(left, right, preferred_element_type=F32)
        return carry

    lax.fori_loop(0, (end - begin + GROUP - 1) // GROUP, group, 0)

    for side in range(2):
        for q in range(4):
            lanes = slice(q * TILE, (q + 1) * TILE)
            mine_ref[side, :, lanes] = acc_ref[side * 8 + core * 4 + q].astype(BF)
            other_ref[side, :, lanes] = acc_ref[side * 8 + (1 - core) * 4 + q].astype(BF)


def tile_products(stage, table, pieces, values):
    width = sum(piece.shape[0] for piece in pieces)
    smem = pl.BlockSpec(memory_space=pltpu.SMEM)
    vmem = pl.BlockSpec(memory_space=pltpu.VMEM)
    return pl.pallas_call(
        functools.partial(tile_kernel, stage),
        in_specs=[smem] + [vmem] * (len(pieces) + 1),
        out_specs=[vmem] * 2,
        scratch_shapes=[pltpu.VMEM((STAGE_COLS + 1, width, TILE), F32)],
        out_shape=[jax.ShapeDtypeStruct((2, width, 512), BF)] * 2,
        compiler_params=pltpu.CompilerParams(vmem_limit_bytes=VMEM_LIMIT),
        cost_estimate=pl.CostEstimate(flops=0, bytes_accessed=1_000_000, transcendentals=0),
    )(table, *pieces, values)


def add_bf(*terms):
    return sum(term.astype(F32) for term in terms).astype(BF)


def spread_kernel(right_ref, left_ref, mine_ref, other_ref, order_ref, weight_ref, grad_ref):
    held = right_ref[...].astype(F32) + left_ref[...].astype(F32)
    held = held + mine_ref[1].astype(F32) + other_ref[1].astype(F32)
    spread = lax.dot_general(
        order_ref[...], held.astype(BF), (((1,), (0,)), ((), ())), preferred_element_type=F32
    ).astype(BF)
    grad_ref[...] = lax.dot_general(
        spread, weight_ref[...], (((0,), (1,)), ((), ())), preferred_element_type=F32
    ).astype(BF)


def finish(right, left, mine, other, order, weight):
    return pl.pallas_call(
        spread_kernel,
        out_shape=jax.ShapeDtypeStruct((right.shape[1], weight.shape[0]), BF),
        compiler_params=pltpu.CompilerParams(vmem_limit_bytes=8 * 1024 * 1024),
        cost_estimate=pl.CostEstimate(flops=0, bytes_accessed=1_000_000, transcendentals=0),
    )(right, left, mine, other, order, weight)


def term_kernel(
    sent_ref,
    left_ref,
    mine_ref,
    other_ref,
    order_ref,
    ahead_ref,
    feat_ref,
    keep_ref,
    give_ref,
    laid_ref,
):
    held = left_ref[...].astype(F32) + mine_ref[1].astype(F32) + other_ref[1].astype(F32)
    both = jnp.concatenate([held.astype(BF), sent_ref[...]], axis=1)
    spread = lax.dot_general(
        order_ref[...], both, (((1,), (0,)), ((), ())), preferred_element_type=F32
    ).astype(BF)
    nodes = jnp.concatenate([feat_ref[...], ahead_ref[...]], axis=0)
    term = lax.dot_general(nodes, spread, (((0,), (1,)), ((), ())), preferred_element_type=F32)
    rows = lax.broadcasted_iota(jnp.int32, (8, TILE), 0)
    spans = lax.broadcasted_iota(jnp.int32, (8, TILE), 1) // 16
    for half in range(2):
        part = term[:, half * TILE : (half + 1) * TILE].reshape(32, 8, TILE)
        moved = jnp.zeros_like(part)
        for step in range(8):
            turned = part
            if step:
                turned = pltpu.roll(pltpu.roll(part, 8 - step, 1), 16 * step, 2)
            keep = ((spans - rows) & 7) == step
            moved = jnp.where(keep[None], turned, moved)
        for r in range(16):
            for upper in range(2):
                laid_ref[
                    r % 2,
                    r // 2 * 16 + half * 8 : r // 2 * 16 + half * 8 + 8,
                    upper * TILE : (upper + 1) * TILE,
                ] = moved[2 * r + upper]
    core = lax.axis_index("row") % 2
    keep_ref[...] = laid_ref[core]
    give_ref[...] = laid_ref[1 - core]


def weight_term(sent, left, mine, other, order, ahead, features):
    vmem = pl.BlockSpec(memory_space=pltpu.VMEM)
    return pl.pallas_call(
        term_kernel,
        in_specs=[vmem] * 7,
        out_specs=[vmem] * 2,
        out_shape=[jax.ShapeDtypeStruct((TILE, 256), F32)] * 2,
        scratch_shapes=[pltpu.VMEM((2, TILE, 256), F32)],
        compiler_params=pltpu.CompilerParams(vmem_limit_bytes=8 * 1024 * 1024),
        cost_estimate=pl.CostEstimate(flops=0, bytes_accessed=1_000_000, transcendentals=0),
    )(sent, left, mine, other, order, ahead, features)


def per_device(features, weight, pre_act, grad_out, tile_ids, tile_count, tile_values):
    pre, grad = pre_act.T, grad_out.T
    masked = jnp.where(pre > 0, grad, jnp.zeros_like(grad))
    half = masked.shape[0] // 2
    along_x = jnp.concatenate(line(shift_x, masked[:half]), axis=0)
    along_y = jnp.concatenate(line(shift_y, masked[half:]), axis=0)

    tile_ids, along_x, along_y, nodes = lax.optimization_barrier(
        (tile_ids, along_x, along_y, features)
    )
    ahead = shift_z(nodes, -1)
    table, order, values = list_pairs(tile_ids, tile_count, tile_values[0, 0])
    pieces = line_by_hops(shift_y, along_x) + line_by_hops(shift_x, along_y)

    table, ahead = lax.optimization_barrier((table, ahead))
    right, left = [], []
    mine, other = tile_products(0, table, pieces, values)
    for stage in range(STAGES - 1):
        other = swap_core(other)
        right = add_bf(*right, mine[0], other[0])
        left = add_bf(*left, mine[1], other[1])
        right, left = [shift_z(right, 1)], [shift_z(left, -1)]
        mine, other = tile_products(stage + 1, table, pieces, values)
    other = swap_core(other)
    sent = add_bf(*right, mine[0], other[0])
    keep, give = weight_term(sent, left[0], mine, other, order, ahead, features)
    blocks = keep + swap_core(give)
    right = shift_z(sent, 1)
    groups = [[i for i in range(256) if i // 16 % 2 == c] for c in range(2)]
    parts = lax.all_to_all(blocks, ("row", "col"), 0, 0, tiled=True, axis_index_groups=groups)
    grad_in = finish(right, left[0], mine, other, order, weight)
    grad_weight = jnp.sum(parts, axis=0).reshape(16, 16)
    return grad_in, grad_weight


def solution(mesh):
    return jax.shard_map(
        per_device,
        mesh=mesh,
        in_specs=(
            P(("col", "row"), None),
            P(),
            P("row", "col"),
            P("row", "col"),
            P("row", "col", None),
            P("row", "col"),
            P("row", "col", None, None, None),
        ),
        out_specs=(P(("col", "row"), None), P("row", "col")),
        check_vma=False,
    )
```

```python
import functools

import jax
import jax.numpy as jnp
from jax import lax
from jax.experimental import pallas as pl
from jax.experimental.pallas import tpu as pltpu
from jax.sharding import PartitionSpec as P

BF = jnp.bfloat16
F32 = jnp.float32
TILE = 128
NX = 4
NY = 4
NZ = 8
COLS = 64
STAGES = 4
STAGE_COLS = COLS // STAGES
GROUP = 8
VMEM_LIMIT = 20 * 1024 * 1024


def shift_x(array, step):
    pairs = [(i, (i // NX) * NX + (i % NX + step) % NX) for i in range(NX * NY)]
    return lax.ppermute(array, "col", pairs)


def shift_y(array, step):
    pairs = [(i, (i + NX * step) % (NX * NY)) for i in range(NX * NY)]
    return lax.ppermute(array, "col", pairs)


def shift_z(array, step):
    pairs = [(i, (i + 2 * step) % (2 * NZ)) for i in range(2 * NZ)]
    return lax.ppermute(array, "row", pairs)


def swap_core(array):
    return lax.ppermute(array, "row", [(i, i ^ 1) for i in range(2 * NZ)])


def line_by_hops(shift, block):
    ahead, behind = shift(block, -1), shift(block, 1)
    half = block.shape[0] // 2
    return block, ahead, shift(behind[:half], 1), shift(ahead[half:], -1), behind


def line(shift, block):
    return block, shift(block, -1), shift(block, 2), shift(block, 1)


def pair_kernel(ids_ref, count_ref, values_hbm, table_ref, order_ref, values_ref, value_sem):
    copy = pltpu.make_async_copy(values_hbm, values_ref, value_sem)
    copy.start()
    slots = ids_ref.shape[1]
    room = table_ref.shape[1]
    ids = jnp.broadcast_to(ids_ref[...], (8, slots))
    slot = lax.broadcasted_iota(jnp.int32, (8, slots), 1)
    live = slot < count_ref[0, 0]
    j = ids & (COLS - 1)
    i = lax.shift_right_logical(ids, 6) & (COLS - 1)
    ahead = (lax.shift_right_logical(j, 3) - lax.axis_index("row") // 2) & (NZ - 1)
    is_right = (ahead >= 1) & (ahead <= 4)
    stage = jnp.where(is_right, 4 - ahead, 3 - ((NZ - ahead) & (NZ - 1)))
    rank = stage * STAGE_COLS + jnp.where(is_right, 0, 8) + (j & 7)
    rank = jnp.where(live, rank, -1)

    def flag(mask):
        return jnp.where(mask, 1.0, 0.0).astype(BF)

    def dot(left, right):
        return jnp.dot(left, right, preferred_element_type=F32)

    columns = lax.broadcasted_iota(jnp.int32, (COLS, slots), 0)
    member = columns == rank[:1]
    before = flag(
        lax.broadcasted_iota(jnp.int32, (slots, slots), 0)
        < lax.broadcasted_iota(jnp.int32, (slots, slots), 1)
    )
    earlier = dot(flag(member), before)
    size = jnp.sum(member.astype(F32), axis=1, keepdims=True)
    pairs = jnp.floor((size + 1.0) * 0.5)
    lower = flag(
        lax.broadcasted_iota(jnp.int32, (COLS, COLS), 1)
        < lax.broadcasted_iota(jnp.int32, (COLS, COLS), 0)
    )
    start = dot(lower, jnp.broadcast_to(pairs, (COLS, TILE)).astype(BF))
    spot = jnp.sum(
        jnp.where(member, earlier + 2.0 * start[:, :1], 0.0), axis=0, keepdims=True
    )
    spot = jnp.where(live[:1], spot, -1.0)
    spot = jnp.broadcast_to(spot, (TILE, slots)).T[:, :1]
    target = 2 * lax.broadcasted_iota(jnp.int32, (slots, room), 1)
    row = lax.broadcasted_iota(jnp.int32, (8, slots), 0)
    facts = jnp.where(row == 0, slot // 16, 0)
    facts = jnp.where(row == 1, slot % 16, facts)
    facts = jnp.where(row == 2, i, facts)
    facts = jnp.where(row == 3, rank & (STAGE_COLS - 1), facts)
    facts = jnp.where(row == 4, 1, facts).astype(F32).astype(BF)
    first = dot(facts, flag(spot == target.astype(F32)))
    second = dot(facts, flag(spot == (target + 1).astype(F32)))

    def code(found):
        return ((found[0:1] * 16.0 + found[1:2]) * COLS + found[2:3]).astype(jnp.int32)

    table_ref[0:1] = code(first)
    table_ref[1:2] = jnp.where(second[4:5] > 0.5, code(second), -1)
    table_ref[2:3] = first[3:4].astype(jnp.int32)
    table_ref[3:4] = jnp.zeros((1, room), jnp.int32)
    table_ref[3:4, :COLS] = start.T[0:1].astype(jnp.int32)
    total = jnp.sum(pairs, axis=0, keepdims=True).astype(jnp.int32)
    table_ref[3:4, TILE : 2 * TILE] = jnp.broadcast_to(total, (1, TILE))

    col = lax.axis_index("col")
    place = lax.broadcasted_iota(jnp.int32, order_ref.shape, 1)
    second = lax.shift_right_logical(place, 7)
    outer, inner = lax.shift_right_logical(place, 5) & 3, lax.shift_right_logical(place, 3) & 3
    dy = jnp.where(second == 0, outer, inner)
    dx = jnp.where(second == 0, inner, outer)
    device = ((col // NX + dy) & (NY - 1)) * NX + ((col % NX + dx) & (NX - 1))
    feature = device * 16 + second * 8 + (place & 7)
    order_ref[...] = flag(lax.broadcasted_iota(jnp.int32, order_ref.shape, 0) == feature)
    copy.wait()


def list_pairs(tile_ids, tile_count, values):
    smem = pl.BlockSpec(memory_space=pltpu.SMEM)
    vmem = pl.BlockSpec(memory_space=pltpu.VMEM)
    room = 256
    return pl.pallas_call(
        pair_kernel,
        in_specs=[vmem, smem, pl.BlockSpec(memory_space=pl.ANY)],
        out_specs=[vmem] * 3,
        out_shape=[
            jax.ShapeDtypeStruct((4, room), jnp.int32),
            jax.ShapeDtypeStruct((256, 256), BF),
            jax.ShapeDtypeStruct(values.shape, BF),
        ],
        scratch_shapes=[pltpu.SemaphoreType.DMA],
        compiler_params=pltpu.CompilerParams(vmem_limit_bytes=16 * 1024 * 1024),
        cost_estimate=pl.CostEstimate(flops=0, bytes_accessed=14_000_000, transcendentals=0),
    )(
        tile_ids.reshape(1, -1),
        tile_count,
        pltpu.with_memory_space_constraint(values, pltpu.HBM),
    )


def tile_kernel(stage, table_ref, *refs):
    *pieces, values_ref, mine_ref, other_ref, acc_ref = refs
    core = lax.axis_index("row") % 2
    width = acc_ref.shape[1]
    begin = table_ref[3, stage * STAGE_COLS]
    end = table_ref[3, (stage + 1) * STAGE_COLS if stage < STAGES - 1 else TILE]

    def clear(j, carry):
        acc_ref[j] = jnp.zeros(acc_ref.shape[1:], F32)
        return carry

    lax.fori_loop(0, STAGE_COLS, clear, 0)

    def gathered(code):
        lanes = pl.ds(pl.multiple_of((code & (COLS - 1)) * TILE, TILE), TILE)
        return jnp.concatenate([piece[:, lanes] for piece in pieces], axis=0)

    def group(g, carry):
        for u in range(GROUP):
            pair = begin + g * GROUP + u
            one, two = table_ref[0, pair], table_ref[1, pair]
            both = two >= 0
            two = jnp.maximum(two, 0)
            left_two = jnp.where(both, gathered(two), jnp.zeros((width, TILE), BF))
            left = jnp.concatenate([gathered(one), left_two], axis=1)
            right = jnp.concatenate(
                [
                    values_ref[lax.shift_right_logical(one, 6)],
                    values_ref[lax.shift_right_logical(two, 6)],
                ],
                axis=0,
            )
            dest = jnp.where(pair < end, table_ref[2, pair], STAGE_COLS)
            acc_ref[dest] += jnp.dot(left, right, preferred_element_type=F32)
        return carry

    lax.fori_loop(0, (end - begin + GROUP - 1) // GROUP, group, 0)

    for side in range(2):
        for q in range(4):
            lanes = slice(q * TILE, (q + 1) * TILE)
            mine_ref[side, :, lanes] = acc_ref[side * 8 + core * 4 + q].astype(BF)
            other_ref[side, :, lanes] = acc_ref[side * 8 + (1 - core) * 4 + q].astype(BF)


def tile_products(stage, table, pieces, values):
    width = sum(piece.shape[0] for piece in pieces)
    smem = pl.BlockSpec(memory_space=pltpu.SMEM)
    vmem = pl.BlockSpec(memory_space=pltpu.VMEM)
    return pl.pallas_call(
        functools.partial(tile_kernel, stage),
        in_specs=[smem] + [vmem] * (len(pieces) + 1),
        out_specs=[vmem] * 2,
        scratch_shapes=[pltpu.VMEM((STAGE_COLS + 1, width, TILE), F32)],
        out_shape=[jax.ShapeDtypeStruct((2, width, 512), BF)] * 2,
        compiler_params=pltpu.CompilerParams(vmem_limit_bytes=VMEM_LIMIT),
        cost_estimate=pl.CostEstimate(flops=0, bytes_accessed=1_000_000, transcendentals=0),
    )(table, *pieces, values)


def add_bf(*terms):
    return sum(term.astype(F32) for term in terms).astype(BF)


def spread_kernel(right_ref, left_ref, mine_ref, other_ref, order_ref, weight_ref, grad_ref):
    held = right_ref[...].astype(F32) + left_ref[...].astype(F32)
    held = held + mine_ref[1].astype(F32) + other_ref[1].astype(F32)
    spread = lax.dot_general(
        order_ref[...], held.astype(BF), (((1,), (0,)), ((), ())), preferred_element_type=F32
    ).astype(BF)
    grad_ref[...] = lax.dot_general(
        spread, weight_ref[...], (((0,), (1,)), ((), ())), preferred_element_type=F32
    ).astype(BF)


def finish(right, left, mine, other, order, weight):
    return pl.pallas_call(
        spread_kernel,
        out_shape=jax.ShapeDtypeStruct((right.shape[1], weight.shape[0]), BF),
        compiler_params=pltpu.CompilerParams(vmem_limit_bytes=8 * 1024 * 1024),
        cost_estimate=pl.CostEstimate(flops=0, bytes_accessed=1_000_000, transcendentals=0),
    )(right, left, mine, other, order, weight)


def term_kernel(
    sent_ref,
    left_ref,
    mine_ref,
    other_ref,
    order_ref,
    ahead_ref,
    feat_ref,
    keep_ref,
    give_ref,
    laid_ref,
):
    held = left_ref[...].astype(F32) + mine_ref[1].astype(F32) + other_ref[1].astype(F32)
    both = jnp.concatenate([held.astype(BF), sent_ref[...]], axis=1)
    spread = lax.dot_general(
        order_ref[...], both, (((1,), (0,)), ((), ())), preferred_element_type=F32
    ).astype(BF)
    nodes = jnp.concatenate([feat_ref[...], ahead_ref[...]], axis=0)
    term = lax.dot_general(nodes, spread, (((0,), (1,)), ((), ())), preferred_element_type=F32)
    rows = lax.broadcasted_iota(jnp.int32, (8, TILE), 0)
    spans = lax.broadcasted_iota(jnp.int32, (8, TILE), 1) // 16
    for half in range(2):
        part = term[:, half * TILE : (half + 1) * TILE].reshape(32, 8, TILE)
        moved = jnp.zeros_like(part)
        for step in range(8):
            turned = part
            if step:
                turned = pltpu.roll(pltpu.roll(part, 8 - step, 1), 16 * step, 2)
            keep = ((spans - rows) & 7) == step
            moved = jnp.where(keep[None], turned, moved)
        for r in range(16):
            for upper in range(2):
                laid_ref[
                    r % 2,
                    r // 2 * 16 + half * 8 : r // 2 * 16 + half * 8 + 8,
                    upper * TILE : (upper + 1) * TILE,
                ] = moved[2 * r + upper]
    core = lax.axis_index("row") % 2
    keep_ref[...] = laid_ref[core]
    give_ref[...] = laid_ref[1 - core]


def weight_term(sent, left, mine, other, order, ahead, features):
    vmem = pl.BlockSpec(memory_space=pltpu.VMEM)
    return pl.pallas_call(
        term_kernel,
        in_specs=[vmem] * 7,
        out_specs=[vmem] * 2,
        out_shape=[jax.ShapeDtypeStruct((TILE, 256), F32)] * 2,
        scratch_shapes=[pltpu.VMEM((2, TILE, 256), F32)],
        compiler_params=pltpu.CompilerParams(vmem_limit_bytes=8 * 1024 * 1024),
        cost_estimate=pl.CostEstimate(flops=0, bytes_accessed=1_000_000, transcendentals=0),
    )(sent, left, mine, other, order, ahead, features)


def per_device(features, weight, pre_act, grad_out, tile_ids, tile_count, tile_values):
    pre, grad = pre_act.T, grad_out.T
    masked = jnp.where(pre > 0, grad, jnp.zeros_like(grad))
    half = masked.shape[0] // 2
    along_x = jnp.concatenate(line(shift_x, masked[:half]), axis=0)
    along_y = jnp.concatenate(line(shift_y, masked[half:]), axis=0)

    tile_ids, along_x, along_y, nodes = lax.optimization_barrier(
        (tile_ids, along_x, along_y, features)
    )
    ahead = shift_z(nodes, -1)
    table, order, values = list_pairs(tile_ids, tile_count, tile_values[0, 0])
    pieces = line_by_hops(shift_y, along_x) + line_by_hops(shift_x, along_y)

    table, ahead = lax.optimization_barrier((table, ahead))
    right, left = [], []
    mine, other = tile_products(0, table, pieces, values)
    for stage in range(STAGES - 1):
        other = swap_core(other)
        right = add_bf(*right, mine[0], other[0])
        left = add_bf(*left, mine[1], other[1])
        right, left = [shift_z(right, 1)], [shift_z(left, -1)]
        mine, other = tile_products(stage + 1, table, pieces, values)
    other = swap_core(other)
    sent = add_bf(*right, mine[0], other[0])
    keep, give = weight_term(sent, left[0], mine, other, order, ahead, features)
    blocks = keep + swap_core(give)
    right = shift_z(sent, 1)
    groups = [[i for i in range(256) if i // 16 % 2 == c] for c in range(2)]
    parts = lax.all_to_all(blocks, ("row", "col"), 0, 0, tiled=True, axis_index_groups=groups)
    grad_in = finish(right, left[0], mine, other, order, weight)
    grad_weight = jnp.sum(parts, axis=0).reshape(16, 16)
    return grad_in, grad_weight


def solution(mesh):
    return jax.shard_map(
        per_device,
        mesh=mesh,
        in_specs=(
            P(("col", "row"), None),
            P(),
            P("row", "col"),
            P("row", "col"),
            P("row", "col", None),
            P("row", "col"),
            P("row", "col", None, None, None),
        ),
        out_specs=(P(("col", "row"), None), P("row", "col")),
        check_vma=False,
    )
```
